128 devices in a mesh: dp: 8 (over y_lo, z), ctx: 16 (over x, y_hi, core).
Axes of the slice: x: 4, y: 4 (y_hi: 2, y_lo: 2; y = y_hi * 2 + y_lo), z: 4, core: 2. Of those that a mesh axis runs over, the one named last changes fastest.
Arguments:
- query_rows: bfloat16 [16, 4096, 2048], P('dp', 'ctx'), may hold values from -6 to 6
- key_rows: bfloat16 [16, 4096, 2048], P('dp', 'ctx'), may hold values from -6 to 6
- value_rows: bfloat16 [16, 4096, 2048], P('dp', 'ctx'), may hold values from -6 to 6
- out_grad: bfloat16 [16, 4096, 2048], P('dp', 'ctx'), may hold values from -6 to 6
- norm_gain: float32 [16, 128], replicated, may hold values from 0.1 to 1.9
- out_weight: bfloat16 [2048, 2048], P(('dp', 'ctx')), may hold values from -0.125 to 0.125
- start_block: int32 [16, 3], P('dp'), may hold values from 0 to 15, as said below
- start_offset: int32 [16, 3], P('dp'), may hold values from 0 to 255
Outputs:
- layer_out: bfloat16 [16, 4096, 2048], P('dp', 'ctx')
- query_grad: bfloat16 [16, 4096, 2048], P('dp', 'ctx')
- key_grad: bfloat16 [16, 4096, 2048], P('dp', 'ctx')
- value_grad: bfloat16 [16, 4096, 2048], P('dp', 'ctx')
- weight_grad: float32 [2048, 2048], P(('dp', 'ctx'))
The draws below stay inside these ranges and needn't reach their ends.
Inputs may be any that keep to these rules, and one draw needn't show every extreme that they name: Position start_block * 256 + start_offset begins a document; the list of a sequence is unordered and may repeat.
All inputs are finite; a program needn't handle non-finite values.
Results may differ from the reference program's by a relative error of at most 0.0053.
Values may be sent and summed in bfloat16 or wider, within the bound.
A program may use at most 192 MiB of HBM per device.

```python
import math
import jax
import jax.numpy as jnp
from jax import lax

BLOCK = 256
H = 16
DH = 128
DW = 2048
BOUNDS = 3
LEN = 4096
SEQS = 16
N_CTX = 16


def boundary_table(key):
    first, second, third, fourth = jax.random.split(key, 4)
    blocks = jax.random.randint(first, (SEQS, BOUNDS), 0, N_CTX)
    offsets = jax.random.randint(second, (SEQS, BOUNDS), 0, BLOCK)
    chosen_row = jax.random.randint(third, (), 0, SEQS)
    chosen_col = jax.random.randint(fourth, (), 0, BOUNDS)
    row_ids = lax.broadcasted_iota(jnp.int32, (SEQS, BOUNDS), 0)
    col_ids = lax.broadcasted_iota(jnp.int32, (SEQS, BOUNDS), 1)
    upper = (row_ids == chosen_row) & (col_ids == chosen_col)
    lower = (row_ids == chosen_row) & (col_ids == (chosen_col + 1) % BOUNDS)
    blocks = jnp.where(upper, N_CTX - 1, jnp.where(lower, 0, blocks))
    offsets = jnp.where(upper, BLOCK - 1, jnp.where(lower, 0, offsets))
    return (blocks.astype(jnp.int32), offsets.astype(jnp.int32))


def draw_start_block(key, part):
    shared = boundary_table(key)
    return shared[0]


def draw_start_offset(key, part):
    shared = boundary_table(key)
    return shared[1]


def block_scale(rng, dims, cuts, low, high):
    def one(axis_at, blocks):
        heights = jax.random.uniform(jax.random.fold_in(jax.random.fold_in(rng, 6), axis_at), (blocks,), jnp.float32, low / len(cuts), high / len(cuts))
        return jnp.repeat(jnp.exp(heights), dims[axis_at] // blocks).reshape((-1,) + (1,) * (len(dims) - axis_at - 1))

    gain = one(*cuts[0])
    for cut in cuts[1:]:
        gain = gain * one(*cut)
    return gain


def gaussian(rng, shape, spread, bound, pieces=(), kind=jnp.bfloat16):
    drawn = spread * jax.random.normal(rng, shape, jnp.float32)
    if pieces:
        drawn = drawn * block_scale(rng, shape, pieces, -0.22, 0.18)
    return jnp.clip(drawn, -bound, bound).astype(kind)


def setup_inputs(seed: int = 0) -> dict:
    key_of = jax.random.split(jax.random.key(seed), 9)
    query_rows = gaussian(key_of[0], (SEQS, LEN, H * DH), 1.0, 6.0, ((0, 8), (1, 16)))
    key_rows = gaussian(key_of[1], (SEQS, LEN, H * DH), 1.0, 6.0, ((0, 8), (1, 16)))
    value_rows = gaussian(key_of[2], (SEQS, LEN, H * DH), 1.0, 6.0, ((0, 8), (1, 16)))
    out_grad = gaussian(key_of[3], (SEQS, LEN, DW), 1.0, 6.0, ((0, 8), (1, 16)))
    norm_gain = jnp.clip(1.0 + 0.18 * jax.random.normal(key_of[4], (H, DH), jnp.float32), 0.1, 1.9)
    out_weight = gaussian(key_of[5], (H * DH, DW), (H * DH) ** -0.5, 0.125, ((0, 128),))
    start_block = draw_start_block(jax.random.fold_in(key_of[8], 71), 0)
    start_offset = draw_start_offset(jax.random.fold_in(key_of[8], 71), 0)
    return dict(query_rows=query_rows, key_rows=key_rows, value_rows=value_rows, out_grad=out_grad, norm_gain=norm_gain, out_weight=out_weight, start_block=start_block, start_offset=start_offset)


exact = lax.Precision.HIGHEST
epsilon = 1.0

def block_masks(doc_block):
    places = jnp.arange(BLOCK, dtype=jnp.int32)
    pre_start = (doc_block == 0).astype(jnp.float32)[:, None, None]
    end_mask = (doc_block == doc_block[-1]).astype(jnp.float32)[:, None, None]
    reset_flag = (doc_block[-1] > 0).astype(jnp.float32)
    causal = (places[:, None] >= places[None, :]) & (doc_block[:, None] == doc_block[None, :])
    return (pre_start, end_mask, reset_flag, causal.astype(jnp.float32)[None])

def rounded(values):
    return values.astype(jnp.bfloat16).astype(jnp.float32)

def one_sequence(query_seq, key_seq, value_seq, grad_seq, block_list, offset_list, norm_gain, out_weight):
    blocks = LEN // BLOCK
    shape5 = (blocks, BLOCK, H, DH)
    positions = jnp.arange(LEN, dtype=jnp.int32)
    start_pos = (block_list * BLOCK + offset_list).astype(jnp.int32)
    starts = jnp.any(positions[:, None] == start_pos[None, :], axis=1)
    local_doc = jnp.cumsum(starts.astype(jnp.int32).reshape(blocks, BLOCK), axis=1).astype(jnp.int32)
    query_f = query_seq.astype(jnp.float32).reshape(shape5)
    key_f = key_seq.astype(jnp.float32).reshape(shape5)
    value_f = value_seq.astype(jnp.float32).reshape(shape5)

    def forward_block(state, items):
        query_b, key_b, value_b, doc_block = items
        pre_start, end_mask, reset_flag, causal = block_masks(doc_block)
        scores = rounded(jnp.einsum('thd,uhd->htu', query_b, key_b, precision=exact) * causal)
        result = jnp.einsum('htu,uhd->thd', scores, value_b, precision=exact)
        result = result + pre_start * jnp.einsum('thd,hde->the', query_b, state, precision=exact)
        fresh = jnp.einsum('thd,the->hde', key_b * end_mask, value_b, precision=exact)
        return (fresh + (1.0 - reset_flag) * state, (result, state))
    zero_state = jnp.zeros((H, DH, DH), jnp.float32)
    _, (att_out, incoming) = lax.scan(forward_block, zero_state, (query_f, key_f, value_f, local_doc))
    att_out = att_out.reshape(LEN, H, DH)
    inv_rms = lax.rsqrt(lax.optimization_barrier(jnp.mean(att_out * att_out, axis=2, keepdims=True)) + epsilon)
    normed = (att_out * inv_rms * norm_gain).astype(jnp.bfloat16).reshape(LEN, H * DH)
    layer_out = jnp.dot(normed, out_weight, preferred_element_type=jnp.float32).astype(jnp.bfloat16)
    normed_grad = jnp.dot(grad_seq, out_weight.T, preferred_element_type=jnp.float32).reshape(LEN, H, DH)
    scaled = normed_grad * norm_gain
    att_grad = inv_rms * (scaled - att_out * inv_rms * inv_rms * lax.optimization_barrier(jnp.mean(scaled * att_out, axis=2, keepdims=True)))
    att_grad = att_grad.astype(jnp.bfloat16)
    grad_f = att_grad.astype(jnp.float32).reshape(shape5)

    def backward_block(carried, items):
        query_b, key_b, value_b, grad_b, doc_block, state = items
        pre_start, end_mask, reset_flag, causal = block_masks(doc_block)
        scores = rounded(jnp.einsum('thd,uhd->htu', query_b, key_b, precision=exact) * causal)
        grad_scores = rounded(jnp.einsum('thd,uhd->htu', grad_b, value_b, precision=exact) * causal)
        query_g = jnp.einsum('htu,uhd->thd', grad_scores, key_b, precision=exact)
        query_g = query_g + pre_start * jnp.einsum('thb,hab->tha', grad_b, state, precision=exact)
        key_g = jnp.einsum('htu,thd->uhd', grad_scores, query_b, precision=exact)
        key_g = key_g + end_mask * jnp.einsum('uhb,hab->uha', value_b, carried, precision=exact)
        value_g = jnp.einsum('htu,thd->uhd', scores, grad_b, precision=exact)
        value_g = value_g + end_mask * jnp.einsum('uha,hab->uhb', key_b, carried, precision=exact)
        fresh = jnp.einsum('thd,the->hde', query_b * pre_start, grad_b, precision=exact)
        return (fresh + (1.0 - reset_flag) * carried, (query_g, key_g, value_g))
    _, (query_g, key_g, value_g) = lax.scan(backward_block, zero_state, (query_f, key_f, value_f, grad_f, local_doc, incoming), reverse=True)
    flat = (LEN, H * DH)
    weight_term = jnp.dot(normed.T, grad_seq, preferred_element_type=jnp.float32)
    return (layer_out, query_g.reshape(flat).astype(jnp.bfloat16), key_g.reshape(flat).astype(jnp.bfloat16), value_g.reshape(flat).astype(jnp.bfloat16), weight_term)

def reference(query_rows, key_rows, value_rows, out_grad, norm_gain, out_weight, start_block, start_offset):

    def per_sequence(total, items):
        results = one_sequence(items[0], items[1], items[2], items[3], items[4], items[5], norm_gain, out_weight)
        return (total + results[4], results[:4])
    initial = jnp.zeros((H * DH, DW), jnp.float32)
    total, (layer_out, query_grad, key_grad, value_grad) = lax.scan(per_sequence, initial, (query_rows, key_rows, value_rows, out_grad, start_block, start_offset))
    weight_grad = total * (1.0 / math.sqrt(SEQS * LEN))
    return (layer_out, query_grad, key_grad, value_grad, weight_grad)
```

```python
import functools
import math

import jax
import jax.numpy as jnp
from jax import lax
from jax.experimental import pallas as pl
from jax.experimental.pallas import tpu as pltpu
from jax.sharding import PartitionSpec as P

BF, F32 = jnp.bfloat16, jnp.float32
MESH = pl.DeviceIdType.MESH
T, H, D, W = 256, 16, 128, 2048
HALF = W // 2
PIECES = ((0, 384, "yxz"), (384, 384, "zyx"), (768, 256, "xzy"))
NT = (((1,), (1,)), ((), ()))
TN = (((0,), (0,)), ((), ()))
NN = (((1,), (0,)), ((), ()))


def dot(a, b, dims):
    return lax.dot_general(a, b, dims, preferred_element_type=F32)


def where_am_i():
    dp, ctx = lax.axis_index("dp"), lax.axis_index("ctx")
    return (ctx // 4, 2 * ((ctx // 2) % 2) + dp // 4, dp % 4, ctx % 2)


def device(at):
    x, y, z, c = at
    return ((y % 2) * 4 + z, (x * 2 + y // 2) * 2 + c)


def moved(at, axis, k):
    x, y, z, c = at
    if axis == "x":
        return ((x + k) % 4, y, z, c)
    if axis == "y":
        return (x, (y + k) % 4, z, c)
    if axis == "z":
        return (x, y, (z + k) % 4, c)
    return (x, y, z, 1 - c)


def chips(ref, at, held, free, cols=None, lead=()):
    x, y, z, _ = at
    every = slice(None)
    parts = (("y", y % 2), ("z", z), ("x", x), ("y", y // 2))
    index = tuple(every if axis in free else place for axis, place in parts if axis in held)
    tail = (every,) if cols is None else (every, cols)
    return ref.at[tuple(lead) + index + tail]


def set_dims(held):
    return tuple(n for axis, n in (("y", 2), ("z", 4), ("x", 4), ("y", 2)) if axis in held)


def remote(src, dst, ssem, rsem, at):
    return pltpu.make_async_remote_copy(
        src_ref=src, dst_ref=dst, send_sem=ssem, recv_sem=rsem, device_id=device(at), device_id_type=MESH
    )


class Scan:
    HOPS = tuple((dx, dh) for dx in range(4) for dh in range(2) if dx or dh)

    def __init__(self, me, backward, fresh, other, tot, arr, car, back, mine, result, send, recv, sb):
        self.me, self.backward = me, backward
        self.fresh, self.other, self.tot, self.arr = fresh, other, tot, arr
        self.car, self.back, self.mine, self.result = car, back, mine, result
        self.send, self.recv, self.sb = send, recv, sb
        x, y, _, c = me
        self.c, self.g = c, x * 2 + y // 2
        self.sib = moved(me, "c", 1)
        self.block = self.g * 2 + c
        self.sib_block = self.g * 2 + 1 - c
        self.second = (c == 0) if backward else (c == 1)

    def keep(self, test):
        hit = test(self.sb[self.c, 0]) | test(self.sb[self.c, 1]) | test(self.sb[self.c, 2])
        return jnp.where(hit, 0.0, 1.0).astype(F32)

    def other_copy(self):
        return remote(self.fresh.at[1 - self.c], self.other, self.send.at[0], self.recv.at[0], self.sib)

    def result_copy(self):
        return remote(self.mine, self.result.at[self.c], self.send.at[1], self.recv.at[1], self.sib)

    def hop(self, i, first, sending):
        dx, dh = self.HOPS[i]
        s = 1 if sending else -1
        at = moved(moved(self.me, "x", s * dx), "y", 2 * dh)
        g = at[0] * 2 + at[1] // 2
        src, dst = (self.tot, self.arr) if first else (self.car, self.back)
        n = 2 + i + (0 if first else 7)
        return remote(src.at[g], dst.at[self.g if sending else g], self.send.at[n], self.recv.at[n], at)

    def begin(self):
        self.other_copy().start()

    def exchange(self):
        self.other_copy().wait_recv()
        mine_keep = self.keep(lambda b: b == self.block)
        sib_keep = self.keep(lambda b: b == self.sib_block)
        a = jnp.where(self.second, 1.0, sib_keep)
        b = jnp.where(self.second, mine_keep, 1.0)

        def one(g, _):
            self.tot[g] = (
                a * self.fresh[self.c, pl.ds(g * 2, 2)] + b * self.other[pl.ds(g * 2, 2)]
            ).astype(BF)
            return 0

        lax.fori_loop(0, 8, one, 0)
        self.arr[self.g] = self.tot[self.g]
        for i in range(7):
            self.hop(i, True, True).start()

    def sum(self):
        for i in range(7):
            self.hop(i, True, False).wait_recv()
        keeps = [self.keep(lambda b, g=g: b // 2 == g) for g in range(8)]
        order = range(7, -1, -1) if self.backward else range(8)
        carried = jnp.zeros((2, D, D), F32)
        for g in order:
            self.car[g] = carried.astype(BF)
            carried = self.arr[g].astype(F32) + keeps[g] * carried
        self.back[self.g] = self.car[self.g]
        for i in range(7):
            self.hop(i, False, True).start()

    def finish(self):
        for i in range(7):
            self.hop(i, False, False).wait_recv()
        mine_keep = self.keep(lambda b: b == self.block)
        sib_keep = self.keep(lambda b: b == self.sib_block)
        a_mine = jnp.where(self.second, 1.0, 0.0).astype(F32)
        b_mine = jnp.where(self.second, sib_keep, 1.0)
        a_sib = jnp.where(self.second, 0.0, 1.0).astype(F32)
        b_sib = jnp.where(self.second, 1.0, mine_keep)

        def one(g, _):
            two = pl.ds(g * 2, 2)
            entering = self.back[g].astype(F32)
            self.mine[two] = (a_sib * self.fresh[self.c, two] + b_sib * entering).astype(BF)
            self.result[self.c, two] = (a_mine * self.other[two] + b_mine * entering).astype(BF)
            return 0

        lax.fori_loop(0, 8, one, 0)
        self.result_copy().start()

    def result_wait(self):
        at = moved(self.me, "c", 1)
        remote(self.mine, self.result.at[1 - self.c], self.send.at[1], self.recv.at[1], at).wait_recv()

    def drain(self):
        self.other_copy().wait_send()
        self.result_copy().wait_send()
        for i in range(7):
            self.hop(i, True, True).wait_send()
            self.hop(i, False, True).wait_send()


def kernel(
    sb, so, gain, q_in, k_in, v_in, g_in, w_in,
    lay_out, qg_out, kg_out, vg_out, dw_out,
    q, k, v, grad, weight, mask, maskt,
    fresh, other, tot, arr, car, back, mine, inc, outg,
    att, vgl, normed, normed_s, grad_s, agrad, lay,
    part, r1a, r1b, r1c, s2a, s2b, s2c, r2a, r2b, r2c, s3a, s3b, s3c, r3a, r3b, r3c, rows, dwv,
    loc, cs, cr, ags, agr, fws, fwr, scs, scr, sds, sdr, rss, rsr,
):
    me = where_am_i()
    x, y, z, c = me
    sib = moved(me, "c", 1)
    block = lax.axis_index("ctx")
    mine_half = pl.multiple_of(c * HALF, HALF)
    sib_half = pl.multiple_of((1 - c) * HALF, HALF)

    loads = [pltpu.make_async_copy(a, b, loc.at[i]) for i, (a, b) in enumerate(((k_in, k), (v_in, v), (q_in, q), (g_in, grad)))]
    for copy in loads:
        copy.start()

    barrier = pltpu.get_barrier_semaphore()
    partners = [sib] + [moved(me, a, n) for a in "xyz" for n in (1, 2, 3)]
    partners += [moved(moved(me, "x", n), "y", 2) for n in (1, 2, 3)]
    for at in partners:
        pl.semaphore_signal(barrier, inc=1, device_id=device(at), device_id_type=MESH)
    pl.semaphore_wait(barrier, len(partners))

    def chip_rows(core, cols):
        return weight.at[y % 2, z, x, y // 2, pl.ds(pl.multiple_of(core * 16, 16), 16), cols]

    w_local = pltpu.make_async_copy(w_in.at[:, pl.ds(mine_half, HALF)], chip_rows(c, pl.ds(mine_half, HALF)), loc.at[4])
    w_local.start()
    w_cross = remote(w_in.at[:, pl.ds(sib_half, HALF)], chip_rows(c, pl.ds(sib_half, HALF)), cs.at[0], cr.at[0], sib)
    w_cross.start()
    g_cross = remote(g_in.at[:, pl.ds(sib_half, HALF)], grad_s, cs.at[1], cr.at[1], sib)

    def cols_of(core, p):
        return pl.ds(pl.multiple_of(core * HALF + PIECES[p][0], 128), PIECES[p][1])

    def gather(phase, p, n, sending):
        order = PIECES[p][2]
        at = me if sending else moved(me, order[phase], -n)
        view = chips(weight, at, "xyz", order[:phase], cols_of(c, p))
        i = (phase * 3 + p) * 3 + n - 1
        to = moved(me, order[phase], n if sending else -n)
        return remote(view, view, ags.at[i], agr.at[i], to)

    def forward(p, n, sending):
        order = PIECES[p][2]
        at = moved(me, order[2], -n)
        view = chips(weight, at, "xyz", order[:2], cols_of(c if sending else 1 - c, p))
        return remote(view, view, fws.at[p * 4 + n], fwr.at[p * 4 + n], sib)

    lows, highs = [], []
    for s in range(2):
        here = [sb[s, j] == block for j in range(3)]
        starts = [jnp.where(here[j], so[s, j], T) for j in range(3)]
        lows.append(jnp.minimum(jnp.minimum(starts[0], starts[1]), starts[2]))
        lasts = [jnp.where(here[j], so[s, j], 0) for j in range(3)]
        highs.append(jnp.maximum(jnp.maximum(lasts[0], lasts[1]), lasts[2]))
        row = lax.broadcasted_iota(jnp.int32, (T, T), 0)
        col = lax.broadcasted_iota(jnp.int32, (T, T), 1)

        def doc(place):
            return sum((place >= start).astype(jnp.int32) for start in starts)

        same = doc(row) == doc(col)
        mask[s] = jnp.where(same & (row >= col), 1.0, 0.0).astype(F32)
        maskt[s] = jnp.where(same & (col >= row), 1.0, 0.0).astype(F32)

    place = lax.broadcasted_iota(jnp.int32, (T, D), 0)

    def before(s):
        return jnp.where(place < lows[s], 1.0, 0.0).astype(F32)

    def ending(s):
        return jnp.where(place >= highs[s], 1.0, 0.0).astype(F32)

    def tile(ref, s, h):
        return ref[s * T:(s + 1) * T, pl.ds(pl.multiple_of(h * D, D), D)]

    def put(ref, s, h, value):
        ref[s * T:(s + 1) * T, pl.ds(pl.multiple_of(h * D, D), D)] = value

    scan_bufs = (fresh, other, tot, arr, car, back, mine)
    ahead = Scan(me, False, *scan_bufs, inc, scs, scr, sb)
    behind = Scan(me, True, *scan_bufs, outg, sds, sdr, sb)

    loads[0].wait()
    loads[1].wait()

    def kv(s):
        def one(h, _):
            keys = (tile(k, s, h).astype(F32) * ending(s)).astype(BF)
            fresh[s, h] = dot(keys, tile(v, s, h), TN)
            return 0

        lax.fori_loop(0, H, one, 0)

    kv(0)
    kv(1)
    ahead.begin()
    g_cross.start()

    w_local.wait()
    w_cross.wait_recv()
    for p in range(3):
        for n in (1, 2, 3):
            gather(0, p, n, True).start()

    loads[2].wait()

    def intra(s):
        def one(h, _):
            scores = (dot(tile(q, s, h), tile(k, s, h), NT) * mask[s]).astype(BF)
            put(att, s, h, dot(scores, tile(v, s, h), NN))
            return 0

        lax.fori_loop(0, H, one, 0)

    ahead.exchange()
    intra(0)
    for p in range(3):
        for n in (1, 2, 3):
            gather(0, p, n, False).wait_recv()
        for n in (1, 2, 3):
            gather(1, p, n, True).start()
    ahead.sum()
    intra(1)
    for p in range(3):
        for n in (1, 2, 3):
            gather(1, p, n, False).wait_recv()
        for n in (1, 2, 3):
            gather(2, p, n, True).start()
        forward(p, 0, True).start()
    ahead.finish()
    for n in (1, 3, 2):
        for p in range(3):
            gather(2, p, n, False).wait_recv()
            forward(p, n, True).start()
    ahead.result_wait()

    def attend(s):
        def one(h, _):
            out = tile(att, s, h) + before(s) * dot(tile(q, s, h), inc[s, h], NN)
            put(att, s, h, out)
            inv = lax.rsqrt(jnp.mean(out * out, axis=1, keepdims=True) + 1.0)
            put(normed, s, h, (out * inv * gain[pl.ds(h, 1), :]).astype(BF))
            return 0

        lax.fori_loop(0, H, one, 0)

    attend(0)
    attend(1)
    n_cross = remote(normed, normed_s, cs.at[2], cr.at[2], sib)
    n_cross.start()
    loads[3].wait()
    for p in range(3):
        for n in range(4):
            forward(p, n, False).wait_recv()

    def gradient(i, _):
        rows_i = weight[i // 4, i % 4].reshape(2 * D, W)
        for s in range(2):
            back_in = dot(grad[s * T:(s + 1) * T, :], rows_i, NT)
            for j in range(2):
                h = i * 2 + j
                out = tile(att, s, h)
                inv = lax.rsqrt(jnp.mean(out * out, axis=1, keepdims=True) + 1.0)
                scaled = back_in[:, j * D:(j + 1) * D] * gain[pl.ds(h, 1), :]
                inner = jnp.mean(scaled * out, axis=1, keepdims=True)
                ag = (inv * (scaled - out * (inv * inv * inner))).astype(BF)
                put(agrad, s, h, ag)
                queries = (tile(q, s, h).astype(F32) * before(s)).astype(BF)
                fresh[s, h] = dot(queries, ag, TN)
        return 0

    ahead.drain()
    lax.fori_loop(0, 8, gradient, 0)
    behind.begin()

    r1, s2, r2 = (r1a, r1b, r1c), (s2a, s2b, s2c), (r2a, r2b, r2c)
    s3, r3 = (s3a, s3b, s3c), (r3a, r3b, r3c)

    def spread(phase, p, n, sending):
        order = PIECES[p][2][::-1]
        to = moved(me, order[phase], n if sending else -n)
        i = (phase * 3 + p) * 3 + n - 1
        free = order[phase + 1:]
        if phase == 0:
            src = chips(part, to, "xyz", free, pl.ds(PIECES[p][0], PIECES[p][1]))
        else:
            src = chips((s2, s3)[phase - 1][p], to, order[phase:], free)
        dst = (r1, r2, r3)[phase][p].at[n - 1]
        return remote(src, dst, rss.at[i], rsr.at[i], to)

    g_cross.wait_recv()
    n_cross.wait_recv()
    for p in range(3):
        first, width, _ = PIECES[p]

        def product(i, _):
            feats = pl.ds(pl.multiple_of(i * 2 * D, 2 * D), 2 * D)
            mine_cols = pl.ds(pl.multiple_of(c * HALF + first, 128), width)
            total = dot(normed[:, feats], grad[:, mine_cols], TN)
            total += dot(normed_s[:, feats], grad_s[:, first:first + width], TN)
            part[i // 4, i % 4, :, :, :, first:first + width] = total.astype(BF).reshape(4, 2, 32, width)
            return 0

        lax.fori_loop(0, 8, product, 0)
        for n in (1, 2, 3):
            spread(0, p, n, True).start()
        if p == 0:
            behind.exchange()

    def project(n, _):
        cols = pl.ds(pl.multiple_of(n * 256, 256), 256)
        lay[:, cols] = dot(normed[...], weight[:, :, :, :, :, cols].reshape(W, 256), NN).astype(BF)
        return 0

    lax.fori_loop(0, 4, project, 0)
    behind.sum()
    lax.fori_loop(4, 8, project, 0)
    lay_copy = pltpu.make_async_copy(lay, lay_out, loc.at[5])
    lay_copy.start()

    def add_up(phase, p):
        order = PIECES[p][2][::-1]
        width = PIECES[p][1]
        for n in (1, 2, 3):
            spread(phase, p, n, False).wait_recv()
        free = order[phase + 1:]
        if phase == 0:
            own = chips(part, me, "xyz", free, pl.ds(PIECES[p][0], width))
        else:
            own = chips((s2, s3)[phase - 1][p], me, order[phase:], free)
        got = (r1, r2, r3)[phase][p]
        dims = set_dims(free)
        if phase == 2:
            total = own[...].astype(F32)
            for n in range(3):
                total += got[n].astype(F32)
            rows[:, PIECES[p][0]:PIECES[p][0] + width] = total
            return
        target = (s2, s3)[phase][p]

        def one(i, _):
            lead, rest = [], i
            for d in dims[::-1]:
                lead = [rest % d] + lead
                rest = rest // d
            lead = tuple(lead)
            total = own[lead].astype(F32)
            for n in range(3):
                total += got[(n,) + lead].astype(F32)
            target[lead] = total.astype(target.dtype)
            return 0

        lax.fori_loop(0, math.prod(dims), one, 0)

    def local_grads(s):
        def one(h, _):
            qh, kh, vh, ah = tile(q, s, h), tile(k, s, h), tile(v, s, h), tile(agrad, s, h)
            ds = (dot(ah, vh, NT) * mask[s]).astype(BF)
            dst = (dot(vh, ah, NT) * maskt[s]).astype(BF)
            st = (dot(kh, qh, NT) * maskt[s]).astype(BF)
            put(att, s, h, dot(dst, qh, NN))
            put(vgl, s, h, dot(st, ah, NN))
            qg = dot(ds, kh, NN) + before(s) * dot(ah, inc[s, h], NT)
            put(q, s, h, qg.astype(BF))
            return 0

        lax.fori_loop(0, H, one, 0)

    local_grads(0)
    behind.finish()
    for p in range(3):
        add_up(0, p)
        for n in (1, 2, 3):
            spread(1, p, n, True).start()
    local_grads(1)
    q_copy = pltpu.make_async_copy(q, qg_out, loc.at[6])
    q_copy.start()
    for p in range(3):
        add_up(1, p)
        for n in (1, 2, 3):
            spread(2, p, n, True).start()
    behind.result_wait()

    def final(s):
        def one(h, _):
            kh, vh, out = tile(k, s, h), tile(v, s, h), outg[s, h]
            kg = tile(att, s, h) + ending(s) * dot(vh, out, NT)
            vg = tile(vgl, s, h) + ending(s) * dot(kh, out, NN)
            put(k, s, h, kg.astype(BF))
            put(v, s, h, vg.astype(BF))
            return 0

        lax.fori_loop(0, H, one, 0)

    final(0)
    final(1)
    k_copy = pltpu.make_async_copy(k, kg_out, loc.at[7])
    k_copy.start()
    v_copy = pltpu.make_async_copy(v, vg_out, loc.at[8])
    v_copy.start()
    for p in range(3):
        add_up(2, p)
    mine_rows = pl.ds(pl.multiple_of(c * 16, 16), 16)
    sib_rows = pl.ds(pl.multiple_of((1 - c) * 16, 16), 16)
    rows[...] = rows[...] * (1.0 / 256.0)
    d_cross = remote(rows.at[sib_rows], dwv.at[:, pl.ds(mine_half, HALF)], cs.at[3], cr.at[3], sib)
    d_cross.start()
    dwv[:, pl.ds(mine_half, HALF)] = rows[mine_rows, :]
    d_back = remote(rows.at[sib_rows], dwv.at[:, pl.ds(sib_half, HALF)], cs.at[3], cr.at[3], sib)
    d_back.wait_recv()
    d_copy = pltpu.make_async_copy(dwv, dw_out, loc.at[9])
    d_copy.start()

    for copy in (w_cross, g_cross, n_cross, d_cross):
        copy.wait_send()
    for p in range(3):
        for n in range(4):
            forward(p, n, True).wait_send()
        for phase in range(3):
            for n in (1, 2, 3):
                gather(phase, p, n, True).wait_send()
                spread(phase, p, n, True).wait_send()
    behind.drain()
    for copy in (lay_copy, q_copy, k_copy, v_copy, d_copy):
        copy.wait()


def per_device(query_rows, key_rows, value_rows, out_grad, norm_gain, out_weight, start_block, start_offset):
    flat = (2 * T, W)
    state = (H, D, D)
    paired = (8, 2, D, D)
    vm = lambda shape, kind: pltpu.VMEM(shape, kind)
    any_space = pl.BlockSpec(memory_space=pl.ANY)
    orders = [(p[2][::-1], p[1]) for p in PIECES]
    r1 = [vm((3,) + set_dims(o[1:]) + (32, w), BF) for o, w in orders]
    s2 = [vm(set_dims(o[1:]) + (32, w), BF) for o, w in orders]
    r2 = [vm((3,) + set_dims(o[2:]) + (32, w), BF) for o, w in orders]
    s3 = [vm(set_dims(o[2:]) + (32, w), F32) for o, w in orders]
    r3 = [vm((3, 32, w), F32) for o, w in orders]
    dma = pltpu.SemaphoreType.DMA
    scratch = (
        [vm(flat, BF)] * 4
        + [vm((2, 4, 4, 2, 32, W), BF), vm((2, T, T), F32), vm((2, T, T), F32)]
        + [vm((2,) + state, F32), vm(state, F32)]
        + [vm(paired, BF)] * 4
        + [vm(state, BF), vm((2,) + state, BF), vm((2,) + state, BF)]
        + [vm(flat, F32), vm(flat, F32), vm(flat, BF), vm(flat, BF), vm((2 * T, HALF), BF), vm(flat, BF), vm(flat, BF)]
        + [vm((2, 4, 4, 2, 32, HALF), BF)]
        + r1 + s2 + r2 + s3 + r3
        + [vm((32, HALF), F32), vm((16, W), F32)]
        + [dma((10,)), dma((4,)), dma((4,)), dma((27,)), dma((27,)), dma((12,)), dma((12,))]
        + [dma((16,)), dma((16,)), dma((16,)), dma((16,)), dma((27,)), dma((27,))]
    )
    smem = pl.BlockSpec(memory_space=pltpu.SMEM)
    outs = pl.pallas_call(
        kernel,
        name="linear_attention",
        out_shape=[jax.ShapeDtypeStruct(flat, BF)] * 4 + [jax.ShapeDtypeStruct((16, W), F32)],
        in_specs=[smem, smem, pl.BlockSpec(memory_space=pltpu.VMEM)] + [any_space] * 5,
        out_specs=[any_space] * 5,
        scratch_shapes=scratch,
        compiler_params=pltpu.CompilerParams(
            collective_id=0, has_side_effects=True, vmem_limit_bytes=60 * 1024 * 1024
        ),
    )(
        start_block, start_offset, norm_gain,
        query_rows.reshape(flat), key_rows.reshape(flat), value_rows.reshape(flat), out_grad.reshape(flat),
        out_weight,
    )
    shape = query_rows.shape
    return tuple(o.reshape(shape) for o in outs[:4]) + (outs[4],)


def solution(mesh):
    rows = P("dp", "ctx", None)
    spread = P(("dp", "ctx"), None)
    return jax.shard_map(
        per_device,
        mesh=mesh,
        in_specs=(rows, rows, rows, rows, P(), spread, P("dp", None), P("dp", None)),
        out_specs=(rows, rows, rows, rows, spread),
        check_vma=False,
    )
```

```python
import functools
import math

import jax
import jax.numpy as jnp
from jax import lax
from jax.experimental import pallas as pl
from jax.experimental.pallas import tpu as pltpu
from jax.sharding import PartitionSpec as P

BF, F32 = jnp.bfloat16, jnp.float32
MESH = pl.DeviceIdType.MESH
T, H, D, W = 256, 16, 128, 2048
HALF = W // 2
PIECES = ((0, 384, "yxz"), (384, 384, "zyx"), (768, 256, "xzy"))
NT = (((1,), (1,)), ((), ()))
TN = (((0,), (0,)), ((), ()))
NN = (((1,), (0,)), ((), ()))


def dot(a, b, dims):
    return lax.dot_general(a, b, dims, preferred_element_type=F32)


def where_am_i():
    dp, ctx = lax.axis_index("dp"), lax.axis_index("ctx")
    return (ctx // 4, 2 * ((ctx // 2) % 2) + dp // 4, dp % 4, ctx % 2)


def device(at):
    x, y, z, c = at
    return ((y % 2) * 4 + z, (x * 2 + y // 2) * 2 + c)


def moved(at, axis, k):
    x, y, z, c = at
    if axis == "x":
        return ((x + k) % 4, y, z, c)
    if axis == "y":
        return (x, (y + k) % 4, z, c)
    if axis == "z":
        return (x, y, (z + k) % 4, c)
    return (x, y, z, 1 - c)


def chips(ref, at, held, free, cols=None, lead=()):
    x, y, z, _ = at
    every = slice(None)
    parts = (("y", y % 2), ("z", z), ("x", x), ("y", y // 2))
    index = tuple(every if axis in free else place for axis, place in parts if axis in held)
    tail = (every,) if cols is None else (every, cols)
    return ref.at[tuple(lead) + index + tail]


def set_dims(held):
    return tuple(n for axis, n in (("y", 2), ("z", 4), ("x", 4), ("y", 2)) if axis in held)


def remote(src, dst, ssem, rsem, at):
    return pltpu.make_async_remote_copy(
        src_ref=src, dst_ref=dst, send_sem=ssem, recv_sem=rsem, device_id=device(at), device_id_type=MESH
    )


class Scan:
    HOPS = tuple((dx, dh) for dx in range(4) for dh in range(2) if dx or dh)

    def __init__(self, me, backward, half, fresh, other, tot, arr, car, back, mine, result, send, recv, sb):
        self.me, self.backward, self.half = me, backward, half
        self.fresh, self.other, self.tot, self.arr = fresh, other, tot, arr
        self.car, self.back, self.mine, self.result = car, back, mine, result
        self.send, self.recv, self.sb = send, recv, sb
        x, y, _, c = me
        self.c, self.g = c, x * 2 + y // 2
        self.sib = moved(me, "c", 1)
        self.block = self.g * 2 + c
        self.sib_block = self.g * 2 + 1 - c
        self.second = (c == 0) if backward else (c == 1)
        self.heads = pl.ds(half * 8, 8)

    def keep(self, test):
        hit = test(self.sb[self.c, 0]) | test(self.sb[self.c, 1]) | test(self.sb[self.c, 2])
        return jnp.where(hit, 0.0, 1.0).astype(F32)

    def pair(self, src, dst, n):
        n += 16 * self.half
        return remote(src, dst, self.send.at[n], self.recv.at[n], self.sib)

    def other_copy(self):
        return self.pair(self.fresh.at[1 - self.c, self.heads], self.other.at[self.heads], 0)

    def result_copy(self, row):
        return self.pair(self.mine.at[self.heads], self.result.at[row, self.heads], 1)

    def hop(self, i, first, sending):
        dx, dh = self.HOPS[i]
        s = 1 if sending else -1
        at = moved(moved(self.me, "x", s * dx), "y", 2 * dh)
        g = at[0] * 2 + at[1] // 2
        src, dst = (self.tot, self.arr) if first else (self.car, self.back)
        n = 16 * self.half + 2 + i + (0 if first else 7)
        return remote(
            src.at[self.half, g], dst.at[self.half, self.g if sending else g], self.send.at[n], self.recv.at[n], at
        )

    def begin(self):
        self.other_copy().start()

    def exchange(self):
        self.other_copy().wait_recv()
        mine_keep = self.keep(lambda b: b == self.block)
        sib_keep = self.keep(lambda b: b == self.sib_block)
        a = jnp.where(self.second, 1.0, sib_keep)
        b = jnp.where(self.second, mine_keep, 1.0)

        def one(i, _):
            for g in (i * 2, i * 2 + 1):
                h = self.half * 8 + g
                self.tot[self.half, g] = (a * self.fresh[self.c, h] + b * self.other[h]).astype(BF)
            return 0

        lax.fori_loop(0, 4, one, 0)
        self.arr[self.half, self.g] = self.tot[self.half, self.g]
        for i in range(7):
            self.hop(i, True, True).start()

    def sum(self):
        for i in range(7):
            self.hop(i, True, False).wait_recv()
        keeps = [self.keep(lambda b, g=g: b // 2 == g) for g in range(8)]
        order = range(7, -1, -1) if self.backward else range(8)
        carried = jnp.zeros((D, D), F32)
        for g in order:
            self.car[self.half, g] = carried.astype(BF)
            carried = self.arr[self.half, g].astype(F32) + keeps[g] * carried
        self.back[self.half, self.g] = self.car[self.half, self.g]
        for i in range(7):
            self.hop(i, False, True).start()

    def finish(self):
        for i in range(7):
            self.hop(i, False, False).wait_recv()
        mine_keep = self.keep(lambda b: b == self.block)
        sib_keep = self.keep(lambda b: b == self.sib_block)
        a_mine = jnp.where(self.second, 1.0, 0.0).astype(F32)
        b_mine = jnp.where(self.second, sib_keep, 1.0)
        a_sib = jnp.where(self.second, 0.0, 1.0).astype(F32)
        b_sib = jnp.where(self.second, 1.0, mine_keep)

        def one(i, _):
            for g in (i * 2, i * 2 + 1):
                h = self.half * 8 + g
                entering = self.back[self.half, g].astype(F32)
                self.mine[h] = (a_sib * self.fresh[self.c, h] + b_sib * entering).astype(BF)
                self.result[self.c, h] = (a_mine * self.other[h] + b_mine * entering).astype(BF)
            return 0

        lax.fori_loop(0, 4, one, 0)
        self.result_copy(self.c).start()

    def result_wait(self):
        self.result_copy(1 - self.c).wait_recv()

    def drain(self):
        self.other_copy().wait_send()
        self.result_copy(self.c).wait_send()
        for i in range(7):
            self.hop(i, True, True).wait_send()
            self.hop(i, False, True).wait_send()


def kernel(
    sb, so, gain, q_in, k_in, v_in, g_in, w_in,
    lay, q, k, v, dwv,
    grad, weight, mask, maskt,
    fresh, other, tot, arr, car, back, mine, inc, outg,
    att, vgl, normed, nt, nts, grad_s, agrad,
    part, r1a, r1b, r1c, s2a, s2b, s2c, r2a, r2b, r2c, s3a, s3b, s3c, r3a, r3b, r3c, rows,
    loc, cs, cr, ags, agr, fws, fwr, scs, scr, sds, sdr, rss, rsr,
):
    me = where_am_i()
    x, y, z, c = me
    sib = moved(me, "c", 1)
    block = lax.axis_index("ctx")
    mine_half = pl.multiple_of(c * HALF, HALF)
    sib_half = pl.multiple_of((1 - c) * HALF, HALF)

    loads = [pltpu.make_async_copy(a, b, loc.at[i]) for i, (a, b) in enumerate(((k_in, k), (v_in, v), (q_in, q), (g_in, grad)))]
    for copy in loads:
        copy.start()

    barrier = pltpu.get_barrier_semaphore()
    partners = [sib] + [moved(me, a, n) for a in "xyz" for n in (1, 2, 3)]
    partners += [moved(moved(me, "x", n), "y", 2) for n in (1, 2, 3)]
    for at in partners:
        pl.semaphore_signal(barrier, inc=1, device_id=device(at), device_id_type=MESH)

    def chip_rows(core, cols):
        return weight.at[y % 2, z, x, y // 2, pl.ds(pl.multiple_of(core * 16, 16), 16), cols]

    w_local = pltpu.make_async_copy(w_in.at[:, pl.ds(mine_half, HALF)], chip_rows(c, pl.ds(mine_half, HALF)), loc.at[4])
    w_local.start()

    def cols_of(core, p):
        return pl.ds(pl.multiple_of(core * HALF + PIECES[p][0], 128), PIECES[p][1])

    def gather(phase, p, n, sending):
        order = PIECES[p][2]
        at = me if sending else moved(me, order[phase], -n)
        view = chips(weight, at, "xyz", order[:phase], cols_of(c, p))
        i = (phase * 3 + p) * 3 + n - 1
        to = moved(me, order[phase], n if sending else -n)
        return remote(view, view, ags.at[i], agr.at[i], to)

    def forward(p, n, sending):
        order = PIECES[p][2]
        at = moved(me, order[2], -n)
        view = chips(weight, at, "xyz", order[:2], cols_of(c if sending else 1 - c, p))
        return remote(view, view, fws.at[p * 4 + n], fwr.at[p * 4 + n], sib)

    lows, highs = [], []
    for s in range(2):
        here = [sb[s, j] == block for j in range(3)]
        starts = [jnp.where(here[j], so[s, j], T) for j in range(3)]
        lows.append(jnp.minimum(jnp.minimum(starts[0], starts[1]), starts[2]))
        lasts = [jnp.where(here[j], so[s, j], 0) for j in range(3)]
        highs.append(jnp.maximum(jnp.maximum(lasts[0], lasts[1]), lasts[2]))
        row = lax.broadcasted_iota(jnp.int32, (T, T), 0)
        col = lax.broadcasted_iota(jnp.int32, (T, T), 1)

        def doc(place):
            return sum((place >= start).astype(jnp.int32) for start in starts)

        same = doc(row) == doc(col)
        mask[s] = jnp.where(same & (row >= col), 1.0, 0.0).astype(F32)
        maskt[s] = jnp.where(same & (col >= row), 1.0, 0.0).astype(F32)

    place = lax.broadcasted_iota(jnp.int32, (T, D), 0)

    def before(s):
        return jnp.where(place < lows[s], 1.0, 0.0).astype(F32)

    def ending(s):
        return jnp.where(place >= highs[s], 1.0, 0.0).astype(F32)

    def tile(ref, s, h):
        return ref[s * T:(s + 1) * T, pl.ds(pl.multiple_of(h * D, D), D)]

    def put(ref, s, h, value):
        ref[s * T:(s + 1) * T, pl.ds(pl.multiple_of(h * D, D), D)] = value

    def over(first, last, step, body):
        def one(i, _):
            body([(s, first + i * step + j) for j in range(step) for s in range(2)])
            return 0

        lax.fori_loop(0, (last - first) // step, one, 0)

    scan_bufs = (fresh, other, tot, arr, car, back, mine)
    ahead = [Scan(me, False, i, *scan_bufs, inc, scs, scr, sb) for i in range(2)]
    behind = [Scan(me, True, i, *scan_bufs, outg, sds, sdr, sb) for i in range(2)]

    def kv(todo):
        keys = [(tile(k, s, h).astype(F32) * ending(s)).astype(BF) for s, h in todo]
        states = [dot(a, tile(v, s, h), TN) for a, (s, h) in zip(keys, todo)]
        for a, (s, h) in zip(states, todo):
            fresh[s, h] = a

    def intra(todo):
        scores = [dot(tile(q, s, h), tile(k, s, h), NT) for s, h in todo]
        scores = [(a * mask[s]).astype(BF) for a, (s, h) in zip(scores, todo)]
        outs = [dot(a, tile(v, s, h), NN) for a, (s, h) in zip(scores, todo)]
        for a, (s, h) in zip(outs, todo):
            put(att, s, h, a)

    def attend(todo):
        outs = [dot(tile(q, s, h), inc[s, h], NN) for s, h in todo]
        outs = [tile(att, s, h) + before(s) * a for a, (s, h) in zip(outs, todo)]
        invs = [lax.rsqrt(jnp.mean(a * a, axis=1, keepdims=True) + 1.0) for a in outs]
        norm = [a * i * gain[pl.ds(h, 1), :] for a, i, (s, h) in zip(outs, invs, todo)]
        for a, n, (s, h) in zip(outs, norm, todo):
            put(att, s, h, a)
            put(normed, s, h, n.astype(BF))
            nt[pl.ds(pl.multiple_of(h * D, D), D), s * T:(s + 1) * T] = n.T.astype(BF)

    def n_cross(half):
        view = pl.ds(half * HALF, HALF)
        return remote(nt.at[view], nts.at[view], cs.at[2 + half], cr.at[2 + half], sib)

    def gradient(i, _):
        rows_i = weight[i // 4, i % 4].reshape(2 * D, W)
        back_in = dot(grad[...], rows_i, NT)
        todo = [(s, j) for j in range(2) for s in range(2)]
        outs = [tile(att, s, i * 2 + j) for s, j in todo]
        invs = [lax.rsqrt(jnp.mean(a * a, axis=1, keepdims=True) + 1.0) for a in outs]
        scaled = [back_in[s * T:(s + 1) * T, j * D:(j + 1) * D] * gain[pl.ds(i * 2 + j, 1), :] for s, j in todo]
        inner = [jnp.mean(a * b, axis=1, keepdims=True) for a, b in zip(scaled, outs)]
        ags_ = [(v_ * (a - b * (v_ * v_ * n))).astype(BF) for v_, a, b, n in zip(invs, scaled, outs, inner)]
        queries = [(tile(q, s, i * 2 + j).astype(F32) * before(s)).astype(BF) for s, j in todo]
        states = [dot(a, b, TN) for a, b in zip(queries, ags_)]
        for a, b, (s, j) in zip(ags_, states, todo):
            put(agrad, s, i * 2 + j, a)
            fresh[s, i * 2 + j] = b
        return 0

    r1, s2, r2 = (r1a, r1b, r1c), (s2a, s2b, s2c), (r2a, r2b, r2c)
    s3, r3 = (s3a, s3b, s3c), (r3a, r3b, r3c)

    def spread(phase, p, n, sending):
        order = PIECES[p][2][::-1]
        to = moved(me, order[phase], n if sending else -n)
        i = (phase * 3 + p) * 3 + n - 1
        free = order[phase + 1:]
        if phase == 0:
            src = chips(part, to, "xyz", free, pl.ds(PIECES[p][0], PIECES[p][1]))
        else:
            src = chips((s2, s3)[phase - 1][p], to, order[phase:], free)
        dst = (r1, r2, r3)[phase][p].at[n - 1]
        return remote(src, dst, rss.at[i], rsr.at[i], to)

    def product(p):
        first, width, _ = PIECES[p]

        def one(i, _):
            feats = pl.ds(pl.multiple_of(i * 512, 512), 512)
            mine_cols = pl.ds(pl.multiple_of(c * HALF + first, 128), width)
            total = dot(nt[feats, :], grad[:, mine_cols], NN)
            total += dot(nts[feats, :], grad_s[:, first:first + width], NN)
            total = total.astype(BF).reshape(2, 4, 2, 32, width)
            for j in range(2):
                part[i // 2, (i % 2) * 2 + j, :, :, :, first:first + width] = total[j]
            return 0

        lax.fori_loop(0, 4, one, 0)
        for n in (1, 2, 3):
            spread(0, p, n, True).start()

    def project(n, _):
        cols = pl.ds(pl.multiple_of(n * 256, 256), 256)
        lay[:, cols] = dot(normed[...], weight[:, :, :, :, :, cols].reshape(W, 256), NN).astype(BF)
        return 0

    def add_up(phase, p):
        order = PIECES[p][2][::-1]
        width = PIECES[p][1]
        for n in (1, 2, 3):
            spread(phase, p, n, False).wait_recv()
        free = order[phase + 1:]
        if phase == 0:
            own = chips(part, me, "xyz", free, pl.ds(PIECES[p][0], width))
        else:
            own = chips((s2, s3)[phase - 1][p], me, order[phase:], free)
        got = (r1, r2, r3)[phase][p]
        dims = set_dims(free)
        if phase == 2:
            total = own[...].astype(F32)
            for n in range(3):
                total += got[n].astype(F32)
            rows[:, PIECES[p][0]:PIECES[p][0] + width] = total * (1.0 / 256.0)
            return
        target = (s2, s3)[phase][p]

        def one(i, _):
            lead, rest = [], i
            for d in dims[::-1]:
                lead = [rest % d] + lead
                rest = rest // d
            lead = tuple(lead)
            total = own[lead].astype(F32)
            for n in range(3):
                total += got[(n,) + lead].astype(F32)
            target[lead] = total.astype(target.dtype)
            return 0

        lax.fori_loop(0, math.prod(dims), one, 0)
        for n in (1, 2, 3):
            spread(phase + 1, p, n, True).start()

    def local_grads(todo):
        ql, kl = [tile(q, s, h) for s, h in todo], [tile(k, s, h) for s, h in todo]
        vl, al = [tile(v, s, h) for s, h in todo], [tile(agrad, s, h) for s, h in todo]
        ds = [dot(a, b, NT) for a, b in zip(al, vl)]
        dst = [dot(b, a, NT) for a, b in zip(al, vl)]
        st = [dot(b, a, NT) for a, b in zip(ql, kl)]
        far = [dot(a, inc[s, h], NT) for a, (s, h) in zip(al, todo)]
        ds = [(a * mask[s]).astype(BF) for a, (s, h) in zip(ds, todo)]
        dst = [(a * maskt[s]).astype(BF) for a, (s, h) in zip(dst, todo)]
        st = [(a * maskt[s]).astype(BF) for a, (s, h) in zip(st, todo)]
        kg = [dot(a, b, NN) for a, b in zip(dst, ql)]
        vg = [dot(a, b, NN) for a, b in zip(st, al)]
        qg = [dot(a, b, NN) + before(s) * f for a, b, f, (s, h) in zip(ds, kl, far, todo)]
        for i, (s, h) in enumerate(todo):
            put(att, s, h, kg[i])
            put(vgl, s, h, vg[i])
            put(q, s, h, qg[i].astype(BF))

    def final(todo):
        kl, vl = [tile(k, s, h) for s, h in todo], [tile(v, s, h) for s, h in todo]
        kg = [dot(a, outg[s, h], NT) for a, (s, h) in zip(vl, todo)]
        vg = [dot(a, outg[s, h], NN) for a, (s, h) in zip(kl, todo)]
        kg = [tile(att, s, h) + ending(s) * a for a, (s, h) in zip(kg, todo)]
        vg = [tile(vgl, s, h) + ending(s) * a for a, (s, h) in zip(vg, todo)]
        for i, (s, h) in enumerate(todo):
            put(k, s, h, kg[i].astype(BF))
            put(v, s, h, vg[i].astype(BF))

    w_cross = remote(w_in.at[:, pl.ds(sib_half, HALF)], chip_rows(c, pl.ds(sib_half, HALF)), cs.at[0], cr.at[0], sib)
    g_cross = remote(g_in.at[:, pl.ds(sib_half, HALF)], grad_s, cs.at[1], cr.at[1], sib)

    def passed(n):
        for p in range(3):
            gather(2, p, n, False).wait_recv()
            forward(p, n, True).start()

    pl.semaphore_wait(barrier, len(partners))
    w_cross.start()
    loads[0].wait()
    loads[1].wait()
    over(0, 8, 2, kv)
    ahead[0].begin()
    w_local.wait()
    w_cross.wait_recv()
    for p in range(3):
        for n in (1, 2, 3):
            gather(0, p, n, True).start()
    over(8, 16, 2, kv)
    ahead[1].begin()
    ahead[0].exchange()
    ahead[1].exchange()
    g_cross.start()
    loads[2].wait()
    over(0, 8, 2, intra)
    for p in range(3):
        for n in (1, 2, 3):
            gather(0, p, n, False).wait_recv()
        for n in (1, 2, 3):
            gather(1, p, n, True).start()
    ahead[0].sum()
    ahead[1].sum()
    over(8, 16, 2, intra)
    for p in range(3):
        for n in (1, 2, 3):
            gather(1, p, n, False).wait_recv()
        for n in (1, 2, 3):
            gather(2, p, n, True).start()
        forward(p, 0, True).start()
    ahead[0].finish()
    ahead[1].finish()
    ahead[0].result_wait()
    over(0, 8, 2, attend)
    n_cross(0).start()
    ahead[1].result_wait()
    over(8, 16, 2, attend)
    n_cross(1).start()
    passed(1)
    loads[3].wait()
    g_cross.wait_recv()
    n_cross(0).wait_recv()
    n_cross(1).wait_recv()
    product(0)
    passed(3)
    product(1)
    passed(2)
    product(2)
    for scan in ahead:
        scan.drain()
    for p in range(3):
        for n in range(4):
            forward(p, n, False).wait_recv()
    lax.fori_loop(0, 4, gradient, 0)
    behind[0].begin()
    lax.fori_loop(4, 8, gradient, 0)
    behind[1].begin()
    behind[0].exchange()
    lax.fori_loop(0, 2, project, 0)
    behind[1].exchange()
    for p in range(3):
        add_up(0, p)
    lax.fori_loop(2, 8, project, 0)
    behind[0].sum()
    behind[1].sum()
    over(0, 8, 2, local_grads)
    for p in range(3):
        add_up(1, p)
    behind[0].finish()
    behind[1].finish()
    over(8, 16, 2, local_grads)
    for p in range(3):
        add_up(2, p)
    mine_rows = pl.ds(pl.multiple_of(c * 16, 16), 16)
    sib_rows = pl.ds(pl.multiple_of((1 - c) * 16, 16), 16)
    d_cross = remote(rows.at[sib_rows], dwv.at[:, pl.ds(mine_half, HALF)], cs.at[4], cr.at[4], sib)
    d_back = remote(rows.at[sib_rows], dwv.at[:, pl.ds(sib_half, HALF)], cs.at[4], cr.at[4], sib)
    d_cross.start()
    dwv[:, pl.ds(mine_half, HALF)] = rows[mine_rows, :]
    behind[0].result_wait()
    over(0, 8, 2, final)
    behind[1].result_wait()
    over(8, 16, 2, final)
    d_back.wait_recv()

    for copy in (w_cross, g_cross, n_cross(0), n_cross(1), d_cross):
        copy.wait_send()
    for p in range(3):
        for n in range(4):
            forward(p, n, True).wait_send()
        for phase in range(3):
            for n in (1, 2, 3):
                gather(phase, p, n, True).wait_send()
                spread(phase, p, n, True).wait_send()
    for scan in behind:
        scan.drain()


def per_device(query_rows, key_rows, value_rows, out_grad, norm_gain, out_weight, start_block, start_offset):
    flat = (2 * T, W)
    state = (H, D, D)
    paired = (2, 8, D, D)
    vm = pltpu.VMEM
    any_space = pl.BlockSpec(memory_space=pl.ANY)
    in_vmem = pl.BlockSpec(memory_space=pltpu.VMEM)
    orders = [(p[2][::-1], p[1]) for p in PIECES]
    r1 = [vm((3,) + set_dims(o[1:]) + (32, w), BF) for o, w in orders]
    s2 = [vm(set_dims(o[1:]) + (32, w), BF) for o, w in orders]
    r2 = [vm((3,) + set_dims(o[2:]) + (32, w), BF) for o, w in orders]
    s3 = [vm(set_dims(o[2:]) + (32, w), F32) for o, w in orders]
    r3 = [vm((3, 32, w), F32) for o, w in orders]
    dma = pltpu.SemaphoreType.DMA
    scratch = (
        [vm(flat, BF)]
        + [vm((2, 4, 4, 2, 32, W), BF), vm((2, T, T), F32), vm((2, T, T), F32)]
        + [vm((2,) + state, F32), vm(state, F32)]
        + [vm(paired, BF)] * 4
        + [vm(state, BF), vm((2,) + state, BF), vm((2,) + state, BF)]
        + [vm(flat, F32), vm(flat, F32), vm(flat, BF), vm((W, 2 * T), BF), vm((W, 2 * T), BF)]
        + [vm((2 * T, HALF), BF), vm(flat, BF)]
        + [vm((2, 4, 4, 2, 32, HALF), BF)]
        + r1 + s2 + r2 + s3 + r3
        + [vm((32, HALF), F32)]
        + [dma((5,)), dma((5,)), dma((5,)), dma((27,)), dma((27,)), dma((12,)), dma((12,))]
        + [dma((32,)), dma((32,)), dma((32,)), dma((32,)), dma((27,)), dma((27,))]
    )
    smem = pl.BlockSpec(memory_space=pltpu.SMEM)
    outs = pl.pallas_call(
        kernel,
        name="linear_attention",
        out_shape=[pltpu.VMEM(flat, BF)] * 4 + [pltpu.VMEM((16, W), F32)],
        in_specs=[smem, smem, in_vmem] + [any_space] * 5,
        out_specs=[in_vmem] * 5,
        scratch_shapes=scratch,
        compiler_params=pltpu.CompilerParams(
            collective_id=0, has_side_effects=True, vmem_limit_bytes=52 * 1024 * 1024
        ),
    )(
        start_block, start_offset, norm_gain,
        query_rows.reshape(flat), key_rows.reshape(flat), value_rows.reshape(flat), out_grad.reshape(flat),
        out_weight,
    )
    shape = query_rows.shape
    return tuple(o.reshape(shape) for o in outs[:4]) + (outs[4],)


def solution(mesh):
    rows = P("dp", "ctx", None)
    spread = P(("dp", "ctx"), None)
    return jax.shard_map(
        per_device,
        mesh=mesh,
        in_specs=(rows, rows, rows, rows, P(), spread, P("dp", None), P("dp", None)),
        out_specs=(rows, rows, rows, rows, spread),
        check_vma=False,
    )
```

```python
import functools
import math

import jax
import jax.numpy as jnp
from jax import lax
from jax.experimental import pallas as pl
from jax.experimental.pallas import tpu as pltpu
from jax.sharding import PartitionSpec as P

BF, F32 = jnp.bfloat16, jnp.float32
MESH = pl.DeviceIdType.MESH
T, H, D, W = 256, 16, 128, 2048
HALF = W // 2
PIECES = ((0, 384, "yxz"), (384, 384, "zyx"), (768, 256, "xzy"))
NT = (((1,), (1,)), ((), ()))
TN = (((0,), (0,)), ((), ()))
NN = (((1,), (0,)), ((), ()))


def dot(a, b, dims):
    return lax.dot_general(a, b, dims, preferred_element_type=F32)


def where_am_i():
    dp, ctx = lax.axis_index("dp"), lax.axis_index("ctx")
    return (ctx // 4, 2 * ((ctx // 2) % 2) + dp // 4, dp % 4, ctx % 2)


def device(at):
    x, y, z, c = at
    return ((y % 2) * 4 + z, (x * 2 + y // 2) * 2 + c)


def moved(at, axis, k):
    x, y, z, c = at
    if axis == "x":
        return ((x + k) % 4, y, z, c)
    if axis == "y":
        return (x, (y + k) % 4, z, c)
    if axis == "z":
        return (x, y, (z + k) % 4, c)
    return (x, y, z, 1 - c)


def chips(ref, at, held, free, cols=None, half=None):
    x, y, z, _ = at
    every = slice(None)
    parts = (("y", y % 2, 2), ("z", z, 4), ("x", x, 4), ("y", y // 2, 2))
    index = []
    for axis, place, size in parts:
        if axis not in held:
            continue
        if axis not in free:
            index.append(place)
        elif half is None:
            index.append(every)
        else:
            index.append(pl.ds(half * size // 2, size // 2))
            half = None
    tail = (every,) if cols is None else (every, cols)
    return ref.at[tuple(index) + tail]


def set_dims(held):
    return tuple(n for axis, n in (("y", 2), ("z", 4), ("x", 4), ("y", 2)) if axis in held)


def remote(src, dst, ssem, rsem, at):
    return pltpu.make_async_remote_copy(
        src_ref=src, dst_ref=dst, send_sem=ssem, recv_sem=rsem, device_id=device(at), device_id_type=MESH
    )


class Scan:
    HOPS = tuple((dx, dh) for dx in range(4) for dh in range(2) if dx or dh)

    def __init__(self, me, backward, half, fresh, other, tot, arr, car, back, mine, result, send, recv, sb):
        self.me, self.backward, self.half = me, backward, half
        self.fresh, self.other, self.tot, self.arr = fresh, other, tot, arr
        self.car, self.back, self.mine, self.result = car, back, mine, result
        self.send, self.recv, self.sb = send, recv, sb
        x, y, _, c = me
        self.c, self.g = c, x * 2 + y // 2
        self.sib = moved(me, "c", 1)
        self.block = self.g * 2 + c
        self.sib_block = self.g * 2 + 1 - c
        self.second = (c == 0) if backward else (c == 1)
        self.heads = pl.ds(half * 8, 8)

    def keep(self, test):
        hit = test(self.sb[self.c, 0]) | test(self.sb[self.c, 1]) | test(self.sb[self.c, 2])
        return jnp.where(hit, 0.0, 1.0).astype(F32)

    def pair(self, src, dst, n):
        n += 16 * self.half
        return remote(src, dst, self.send.at[n], self.recv.at[n], self.sib)

    def other_copy(self):
        return self.pair(self.fresh.at[1 - self.c, self.heads], self.other.at[self.heads], 0)

    def result_copy(self, row):
        return self.pair(self.mine.at[self.heads], self.result.at[row, self.heads], 1)

    def hop(self, i, first, sending):
        dx, dh = self.HOPS[i]
        s = 1 if sending else -1
        at = moved(moved(self.me, "x", s * dx), "y", 2 * dh)
        g = at[0] * 2 + at[1] // 2
        src, dst = (self.tot, self.arr) if first else (self.car, self.back)
        n = 16 * self.half + 2 + i + (0 if first else 7)
        return remote(
            src.at[self.half, g], dst.at[self.half, self.g if sending else g], self.send.at[n], self.recv.at[n], at
        )

    def begin(self):
        self.other_copy().start()

    def exchange(self):
        self.other_copy().wait_recv()
        mine_keep = self.keep(lambda b: b == self.block)
        sib_keep = self.keep(lambda b: b == self.sib_block)
        a = jnp.where(self.second, 1.0, sib_keep)
        b = jnp.where(self.second, mine_keep, 1.0)

        def one(i, _):
            for g in (i * 2, i * 2 + 1):
                h = self.half * 8 + g
                self.tot[self.half, g] = (a * self.fresh[self.c, h] + b * self.other[h]).astype(BF)
            return 0

        lax.fori_loop(0, 4, one, 0)
        self.arr[self.half, self.g] = self.tot[self.half, self.g]
        for i in range(7):
            self.hop(i, True, True).start()

    def sum(self):
        for i in range(7):
            self.hop(i, True, False).wait_recv()
        keeps = [self.keep(lambda b, g=g: b // 2 == g) for g in range(8)]
        order = range(7, -1, -1) if self.backward else range(8)
        carried = jnp.zeros((D, D), F32)
        for g in order:
            self.car[self.half, g] = carried.astype(BF)
            carried = self.arr[self.half, g].astype(F32) + keeps[g] * carried
        self.back[self.half, self.g] = self.car[self.half, self.g]
        for i in range(7):
            self.hop(i, False, True).start()

    def finish(self):
        for i in range(7):
            self.hop(i, False, False).wait_recv()
        mine_keep = self.keep(lambda b: b == self.block)
        sib_keep = self.keep(lambda b: b == self.sib_block)
        a_mine = jnp.where(self.second, 1.0, 0.0).astype(F32)
        b_mine = jnp.where(self.second, sib_keep, 1.0)
        a_sib = jnp.where(self.second, 0.0, 1.0).astype(F32)
        b_sib = jnp.where(self.second, 1.0, mine_keep)

        def one(i, _):
            for g in (i * 2, i * 2 + 1):
                h = self.half * 8 + g
                entering = self.back[self.half, g].astype(F32)
                self.mine[h] = (a_sib * self.fresh[self.c, h] + b_sib * entering).astype(BF)
                self.result[self.c, h] = (a_mine * self.other[h] + b_mine * entering).astype(BF)
            return 0

        lax.fori_loop(0, 4, one, 0)
        self.result_copy(self.c).start()

    def result_wait(self):
        self.result_copy(1 - self.c).wait_recv()

    def drain(self):
        self.other_copy().wait_send()
        self.result_copy(self.c).wait_send()
        for i in range(7):
            self.hop(i, True, True).wait_send()
            self.hop(i, False, True).wait_send()


def kernel(
    sb, so, gain, q_in, k_in, v_in, g_in, w_in,
    lay, q, k, v, dwv,
    grad, weight, mask, maskt,
    fresh, other, tot, arr, car, back, mine, inc, outg,
    att, vgl, normed, nt, nts, grad_s, agrad,
    part, r1a, r1b, r1c, s2a, s2b, s2c, r2a, r2b, r2c, s3a, s3b, s3c, r3a, r3b, r3c, rows,
    loc, cs, cr, ags, agr, fws, fwr, scs, scr, sds, sdr, rss, rsr,
):
    me = where_am_i()
    x, y, z, c = me
    sib = moved(me, "c", 1)
    block = lax.axis_index("ctx")
    mine_half = pl.multiple_of(c * HALF, HALF)
    sib_half = pl.multiple_of((1 - c) * HALF, HALF)

    loads = [pltpu.make_async_copy(a, b, loc.at[i]) for i, (a, b) in enumerate(((k_in, k), (v_in, v), (q_in, q), (g_in, grad)))]
    for copy in loads:
        copy.start()

    barrier = pltpu.get_barrier_semaphore()
    partners = [sib] + [moved(me, a, n) for a in "xyz" for n in (1, 2, 3)]
    partners += [moved(moved(me, "x", n), "y", 2) for n in (1, 2, 3)]
    for at in partners:
        pl.semaphore_signal(barrier, inc=1, device_id=device(at), device_id_type=MESH)

    def chip_rows(core, cols):
        return weight.at[y % 2, z, x, y // 2, pl.ds(pl.multiple_of(core * 16, 16), 16), cols]

    w_local = pltpu.make_async_copy(w_in.at[:, pl.ds(mine_half, HALF)], chip_rows(c, pl.ds(mine_half, HALF)), loc.at[4])
    w_local.start()

    def cols_of(core, p):
        return pl.ds(pl.multiple_of(core * HALF + PIECES[p][0], 128), PIECES[p][1])

    def gather(phase, p, n, sending):
        order = PIECES[p][2]
        at = me if sending else moved(me, order[phase], -n)
        view = chips(weight, at, "xyz", order[:phase], cols_of(c, p))
        i = (phase * 3 + p) * 3 + n - 1
        to = moved(me, order[phase], n if sending else -n)
        return remote(view, view, ags.at[i], agr.at[i], to)

    def forward(p, n, sending):
        order = PIECES[p][2]
        at = moved(me, order[2], -n)
        view = chips(weight, at, "xyz", order[:2], cols_of(c if sending else 1 - c, p))
        return remote(view, view, fws.at[p * 4 + n], fwr.at[p * 4 + n], sib)

    lows, highs = [], []
    for s in range(2):
        here = [sb[s, j] == block for j in range(3)]
        starts = [jnp.where(here[j], so[s, j], T) for j in range(3)]
        lows.append(jnp.minimum(jnp.minimum(starts[0], starts[1]), starts[2]))
        lasts = [jnp.where(here[j], so[s, j], 0) for j in range(3)]
        highs.append(jnp.maximum(jnp.maximum(lasts[0], lasts[1]), lasts[2]))
        row = lax.broadcasted_iota(jnp.int32, (T, T), 0)
        col = lax.broadcasted_iota(jnp.int32, (T, T), 1)

        def doc(place):
            return sum((place >= start).astype(jnp.int32) for start in starts)

        same = doc(row) == doc(col)
        mask[s] = jnp.where(same & (row >= col), 1.0, 0.0).astype(F32)
        maskt[s] = jnp.where(same & (col >= row), 1.0, 0.0).astype(F32)

    place = lax.broadcasted_iota(jnp.int32, (T, D), 0)

    def before(s):
        return jnp.where(place < lows[s], 1.0, 0.0).astype(F32)

    def ending(s):
        return jnp.where(place >= highs[s], 1.0, 0.0).astype(F32)

    def tile(ref, s, h):
        return ref[s * T:(s + 1) * T, pl.ds(pl.multiple_of(h * D, D), D)]

    def put(ref, s, h, value):
        ref[s * T:(s + 1) * T, pl.ds(pl.multiple_of(h * D, D), D)] = value

    def over(first, last, step, body):
        def one(i, _):
            body([(s, first + i * step + j) for j in range(step) for s in range(2)])
            return 0

        lax.fori_loop(0, (last - first) // step, one, 0)

    scan_bufs = (fresh, other, tot, arr, car, back, mine)
    ahead = [Scan(me, False, i, *scan_bufs, inc, scs, scr, sb) for i in range(2)]
    behind = [Scan(me, True, i, *scan_bufs, outg, sds, sdr, sb) for i in range(2)]

    def kv(todo):
        keys = [(tile(k, s, h).astype(F32) * ending(s)).astype(BF) for s, h in todo]
        states = [dot(a, tile(v, s, h), TN) for a, (s, h) in zip(keys, todo)]
        for a, (s, h) in zip(states, todo):
            fresh[s, h] = a

    def intra(todo):
        scores = [dot(tile(q, s, h), tile(k, s, h), NT) for s, h in todo]
        scores = [(a * mask[s]).astype(BF) for a, (s, h) in zip(scores, todo)]
        outs = [dot(a, tile(v, s, h), NN) for a, (s, h) in zip(scores, todo)]
        for a, (s, h) in zip(outs, todo):
            put(att, s, h, a)

    def attend(todo):
        outs = [dot(tile(q, s, h), inc[s, h], NN) for s, h in todo]
        outs = [tile(att, s, h) + before(s) * a for a, (s, h) in zip(outs, todo)]
        invs = [lax.rsqrt(jnp.mean(a * a, axis=1, keepdims=True) + 1.0) for a in outs]
        norm = [a * i * gain[pl.ds(h, 1), :] for a, i, (s, h) in zip(outs, invs, todo)]
        for a, n, (s, h) in zip(outs, norm, todo):
            put(att, s, h, a)
            put(normed, s, h, n.astype(BF))
            nt[pl.ds(pl.multiple_of(h * D, D), D), s * T:(s + 1) * T] = n.T.astype(BF)

    def n_cross(half):
        view = pl.ds(half * HALF, HALF)
        return remote(nt.at[view], nts.at[view], cs.at[2 + half], cr.at[2 + half], sib)

    def gradient(i, _):
        rows_i = weight[i // 4, i % 4].reshape(2 * D, W)
        back_in = dot(grad[...], rows_i, NT)
        todo = [(s, j) for j in range(2) for s in range(2)]
        outs = [tile(att, s, i * 2 + j) for s, j in todo]
        invs = [lax.rsqrt(jnp.mean(a * a, axis=1, keepdims=True) + 1.0) for a in outs]
        scaled = [back_in[s * T:(s + 1) * T, j * D:(j + 1) * D] * gain[pl.ds(i * 2 + j, 1), :] for s, j in todo]
        inner = [jnp.mean(a * b, axis=1, keepdims=True) for a, b in zip(scaled, outs)]
        ags_ = [(v_ * (a - b * (v_ * v_ * n))).astype(BF) for v_, a, b, n in zip(invs, scaled, outs, inner)]
        queries = [(tile(q, s, i * 2 + j).astype(F32) * before(s)).astype(BF) for s, j in todo]
        states = [dot(a, b, TN) for a, b in zip(queries, ags_)]
        for a, b, (s, j) in zip(ags_, states, todo):
            put(agrad, s, i * 2 + j, a)
            fresh[s, i * 2 + j] = b
        return 0

    r1, s2, r2 = (r1a, r1b, r1c), (s2a, s2b, s2c), (r2a, r2b, r2c)
    s3, r3 = (s3a, s3b, s3c), (r3a, r3b, r3c)

    def spread(phase, p, n, sending):
        order = PIECES[p][2][::-1]
        to = moved(me, order[phase], n if sending else -n)
        i = (phase * 3 + p) * 3 + n - 1
        free = order[phase + 1:]
        if phase == 0:
            src = chips(part, to, "xyz", free, pl.ds(PIECES[p][0], PIECES[p][1]))
        else:
            src = chips((s2, s3)[phase - 1][p], to, order[phase:], free)
        dst = (r1, r2, r3)[phase][p].at[n - 1]
        return remote(src, dst, rss.at[i], rsr.at[i], to)

    def first_step(p, kind, n, sending):
        order = PIECES[p][2][::-1]
        side = 0 if n == 1 else 1
        half = 1 - side if kind == 1 else side
        axis, free = order[0], order[1:]
        whose = moved(me, axis, 2 if kind == 0 else n)
        src = chips(part, whose, "xyz", free, pl.ds(PIECES[p][0], PIECES[p][1]), half)
        size = set_dims(free)[0] // 2
        dst = r1[p].at[1 if kind == 0 else n - 1, pl.ds(half * size, size)]
        i = 27 + (kind * 2 + side) * 3 + p
        to = moved(me, axis, n if sending else -n)
        return remote(src, dst, rss.at[i], rsr.at[i], to)

    def combine(p):
        order = PIECES[p][2][::-1]
        free = order[1:]
        dims = set_dims(free)
        dims = (dims[0] // 2,) + dims[1:]
        for n in (1, 3):
            first_step(p, 0, n, False).wait_recv()
            half = 0 if n == 1 else 1
            own = chips(part, moved(me, order[0], n), "xyz", free, pl.ds(PIECES[p][0], PIECES[p][1]), half)
            got = r1[p].at[1, pl.ds(half * dims[0], dims[0])]

            def one(i, _):
                lead, rest = [], i
                for d in dims[::-1]:
                    lead = [rest % d] + lead
                    rest = rest // d
                lead = tuple(lead)
                own[lead] = (own[lead].astype(F32) + got[lead].astype(F32)).astype(BF)
                return 0

            lax.fori_loop(0, math.prod(dims), one, 0)
            first_step(p, 2, n, True).start()

    def product(p):
        first, width, _ = PIECES[p]

        def one(i, _):
            feats = pl.ds(pl.multiple_of(i * 512, 512), 512)
            mine_cols = pl.ds(pl.multiple_of(c * HALF + first, 128), width)
            total = dot(nt[feats, :], grad[:, mine_cols], NN)
            total += dot(nts[feats, :], grad_s[:, first:first + width], NN)
            total = total.astype(BF).reshape(2, 4, 2, 32, width)
            for j in range(2):
                part[i // 2, (i % 2) * 2 + j, :, :, :, first:first + width] = total[j]
            return 0

        lax.fori_loop(0, 4, one, 0)
        for kind in (0, 1):
            for n in (1, 3):
                first_step(p, kind, n, True).start()

    def project(n, _):
        cols = pl.ds(pl.multiple_of(n * 256, 256), 256)
        lay[:, cols] = dot(normed[...], weight[:, :, :, :, :, cols].reshape(W, 256), NN).astype(BF)
        return 0

    def add_up(phase, p):
        order = PIECES[p][2][::-1]
        width = PIECES[p][1]
        if phase == 0:
            for n in (1, 3):
                first_step(p, 1, n, False).wait_recv()
                first_step(p, 2, n, False).wait_recv()
        else:
            for n in (1, 2, 3):
                spread(phase, p, n, False).wait_recv()
        terms = (0, 2) if phase == 0 else (0, 1, 2)
        free = order[phase + 1:]
        if phase == 0:
            own = chips(part, me, "xyz", free, pl.ds(PIECES[p][0], width))
        else:
            own = chips((s2, s3)[phase - 1][p], me, order[phase:], free)
        got = (r1, r2, r3)[phase][p]
        dims = set_dims(free)
        if phase == 2:
            total = own[...].astype(F32)
            for n in terms:
                total += got[n].astype(F32)
            rows[:, PIECES[p][0]:PIECES[p][0] + width] = total * (1.0 / 256.0)
            return
        target = (s2, s3)[phase][p]

        def one(i, _):
            lead, rest = [], i
            for d in dims[::-1]:
                lead = [rest % d] + lead
                rest = rest // d
            lead = tuple(lead)
            total = own[lead].astype(F32)
            for n in terms:
                total += got[(n,) + lead].astype(F32)
            target[lead] = total.astype(target.dtype)
            return 0

        lax.fori_loop(0, math.prod(dims), one, 0)
        for n in (1, 2, 3):
            spread(phase + 1, p, n, True).start()

    def local_grads(todo):
        ql, kl = [tile(q, s, h) for s, h in todo], [tile(k, s, h) for s, h in todo]
        vl, al = [tile(v, s, h) for s, h in todo], [tile(agrad, s, h) for s, h in todo]
        ds = [dot(a, b, NT) for a, b in zip(al, vl)]
        dst = [dot(b, a, NT) for a, b in zip(al, vl)]
        st = [dot(b, a, NT) for a, b in zip(ql, kl)]
        far = [dot(a, inc[s, h], NT) for a, (s, h) in zip(al, todo)]
        ds = [(a * mask[s]).astype(BF) for a, (s, h) in zip(ds, todo)]
        dst = [(a * maskt[s]).astype(BF) for a, (s, h) in zip(dst, todo)]
        st = [(a * maskt[s]).astype(BF) for a, (s, h) in zip(st, todo)]
        kg = [dot(a, b, NN) for a, b in zip(dst, ql)]
        vg = [dot(a, b, NN) for a, b in zip(st, al)]
        qg = [dot(a, b, NN) + before(s) * f for a, b, f, (s, h) in zip(ds, kl, far, todo)]
        for i, (s, h) in enumerate(todo):
            put(att, s, h, kg[i])
            put(vgl, s, h, vg[i])
            put(q, s, h, qg[i].astype(BF))

    def final(todo):
        kl, vl = [tile(k, s, h) for s, h in todo], [tile(v, s, h) for s, h in todo]
        kg = [dot(a, outg[s, h], NT) for a, (s, h) in zip(vl, todo)]
        vg = [dot(a, outg[s, h], NN) for a, (s, h) in zip(kl, todo)]
        kg = [tile(att, s, h) + ending(s) * a for a, (s, h) in zip(kg, todo)]
        vg = [tile(vgl, s, h) + ending(s) * a for a, (s, h) in zip(vg, todo)]
        for i, (s, h) in enumerate(todo):
            put(k, s, h, kg[i].astype(BF))
            put(v, s, h, vg[i].astype(BF))

    w_cross = remote(w_in.at[:, pl.ds(sib_half, HALF)], chip_rows(c, pl.ds(sib_half, HALF)), cs.at[0], cr.at[0], sib)
    g_cross = remote(g_in.at[:, pl.ds(sib_half, HALF)], grad_s, cs.at[1], cr.at[1], sib)

    def passed(n):
        for p in range(3):
            gather(2, p, n, False).wait_recv()
            forward(p, n, True).start()

    loads[0].wait()
    loads[1].wait()
    over(0, 8, 2, kv)
    pl.semaphore_wait(barrier, len(partners))
    w_cross.start()
    ahead[0].begin()
    w_local.wait()
    w_cross.wait_recv()
    for p in range(3):
        for n in (1, 2, 3):
            gather(0, p, n, True).start()
    over(8, 16, 2, kv)
    ahead[1].begin()
    ahead[0].exchange()
    ahead[1].exchange()
    g_cross.start()
    loads[2].wait()
    over(0, 8, 2, intra)
    for p in range(3):
        for n in (1, 2, 3):
            gather(0, p, n, False).wait_recv()
        for n in (1, 2, 3):
            gather(1, p, n, True).start()
    ahead[0].sum()
    ahead[1].sum()
    over(8, 16, 2, intra)
    for p in range(3):
        for n in (1, 2, 3):
            gather(1, p, n, False).wait_recv()
        for n in (1, 2, 3):
            gather(2, p, n, True).start()
        forward(p, 0, True).start()
    ahead[0].finish()
    ahead[1].finish()
    ahead[0].result_wait()
    over(0, 8, 2, attend)
    n_cross(0).start()
    ahead[1].result_wait()
    over(8, 16, 2, attend)
    n_cross(1).start()
    passed(1)
    loads[3].wait()
    g_cross.wait_recv()
    n_cross(0).wait_recv()
    n_cross(1).wait_recv()
    product(0)
    passed(3)
    product(1)
    passed(2)
    product(2)
    for scan in ahead:
        scan.drain()
    for p in range(3):
        for n in range(4):
            forward(p, n, False).wait_recv()
    lax.fori_loop(0, 4, gradient, 0)
    behind[0].begin()
    combine(0)
    combine(1)
    lax.fori_loop(4, 8, gradient, 0)
    behind[1].begin()
    combine(2)
    behind[0].exchange()
    lax.fori_loop(0, 2, project, 0)
    behind[1].exchange()
    for p in range(3):
        add_up(0, p)
    lax.fori_loop(2, 8, project, 0)
    behind[0].sum()
    behind[1].sum()
    over(0, 8, 2, local_grads)
    for p in range(3):
        add_up(1, p)
    behind[0].finish()
    behind[1].finish()
    over(8, 16, 2, local_grads)
    for p in range(3):
        add_up(2, p)
    mine_rows = pl.ds(pl.multiple_of(c * 16, 16), 16)
    sib_rows = pl.ds(pl.multiple_of((1 - c) * 16, 16), 16)
    d_cross = remote(rows.at[sib_rows], dwv.at[:, pl.ds(mine_half, HALF)], cs.at[4], cr.at[4], sib)
    d_back = remote(rows.at[sib_rows], dwv.at[:, pl.ds(sib_half, HALF)], cs.at[4], cr.at[4], sib)
    d_cross.start()
    dwv[:, pl.ds(mine_half, HALF)] = rows[mine_rows, :]
    behind[0].result_wait()
    over(0, 8, 2, final)
    behind[1].result_wait()
    over(8, 16, 2, final)
    d_back.wait_recv()

    for copy in (w_cross, g_cross, n_cross(0), n_cross(1), d_cross):
        copy.wait_send()
    for p in range(3):
        for n in range(4):
            forward(p, n, True).wait_send()
        for phase in range(3):
            for n in (1, 2, 3):
                gather(phase, p, n, True).wait_send()
                if phase:
                    spread(phase, p, n, True).wait_send()
        for n in (1, 3):
            for kind in range(3):
                first_step(p, kind, n, True).wait_send()
    for scan in behind:
        scan.drain()


def per_device(query_rows, key_rows, value_rows, out_grad, norm_gain, out_weight, start_block, start_offset):
    flat = (2 * T, W)
    state = (H, D, D)
    paired = (2, 8, D, D)
    vm = pltpu.VMEM
    any_space = pl.BlockSpec(memory_space=pl.ANY)
    in_vmem = pl.BlockSpec(memory_space=pltpu.VMEM)
    orders = [(p[2][::-1], p[1]) for p in PIECES]
    r1 = [vm((3,) + set_dims(o[1:]) + (32, w), BF) for o, w in orders]
    s2 = [vm(set_dims(o[1:]) + (32, w), BF) for o, w in orders]
    r2 = [vm((3,) + set_dims(o[2:]) + (32, w), BF) for o, w in orders]
    s3 = [vm(set_dims(o[2:]) + (32, w), F32) for o, w in orders]
    r3 = [vm((3, 32, w), F32) for o, w in orders]
    dma = pltpu.SemaphoreType.DMA
    scratch = (
        [vm(flat, BF)]
        + [vm((2, 4, 4, 2, 32, W), BF), vm((2, T, T), F32), vm((2, T, T), F32)]
        + [vm((2,) + state, F32), vm(state, F32)]
        + [vm(paired, BF)] * 4
        + [vm(state, BF), vm((2,) + state, BF), vm((2,) + state, BF)]
        + [vm(flat, F32), vm(flat, F32), vm(flat, BF), vm((W, 2 * T), BF), vm((W, 2 * T), BF)]
        + [vm((2 * T, HALF), BF), vm(flat, BF)]
        + [vm((2, 4, 4, 2, 32, HALF), BF)]
        + r1 + s2 + r2 + s3 + r3
        + [vm((32, HALF), F32)]
        + [dma((5,)), dma((5,)), dma((5,)), dma((27,)), dma((27,)), dma((12,)), dma((12,))]
        + [dma((32,)), dma((32,)), dma((32,)), dma((32,)), dma((45,)), dma((45,))]
    )
    smem = pl.BlockSpec(memory_space=pltpu.SMEM)
    outs = pl.pallas_call(
        kernel,
        name="linear_attention",
        out_shape=[pltpu.VMEM(flat, BF)] * 4 + [pltpu.VMEM((16, W), F32)],
        in_specs=[smem, smem, in_vmem] + [any_space] * 5,
        out_specs=[in_vmem] * 5,
        scratch_shapes=scratch,
        compiler_params=pltpu.CompilerParams(
            collective_id=0, has_side_effects=True, vmem_limit_bytes=52 * 1024 * 1024
        ),
    )(
        start_block, start_offset, norm_gain,
        query_rows.reshape(flat), key_rows.reshape(flat), value_rows.reshape(flat), out_grad.reshape(flat),
        out_weight,
    )
    shape = query_rows.shape
    return tuple(o.reshape(shape) for o in outs[:4]) + (outs[4],)


def solution(mesh):
    rows = P("dp", "ctx", None)
    spread = P(("dp", "ctx"), None)
    return jax.shard_map(
        per_device,
        mesh=mesh,
        in_specs=(rows, rows, rows, rows, P(), spread, P("dp", None), P("dp", None)),
        out_specs=(rows, rows, rows, rows, spread),
        check_vma=False,
    )
```
